32 devices in a mesh: fsdp: 16 (over z, x, core), tok: 2 (over y).
Axes of the slice: x: 2, y: 2, z: 4, core: 2. Of those that a mesh axis runs over, the one named last changes fastest.
Arguments:
- tokens: bfloat16 [2048, 2048], P('fsdp', 'tok'), may hold values from -6 to 6
- expert_ids: int32 [2048, 4], P('fsdp'), may hold values from 0 to 31, all different within a row; in each aligned block of 128 rows (0 to 127, 128 to 255, ...) at most 32 rows name the same one
- gate_probs: float32 [2048, 4], P('fsdp'), may hold values from 0.05 to 1
- w_gate: bfloat16 [32, 1408, 2048], P('fsdp', 'tok'), may hold values from -0.125 to 0.125
- w_up: bfloat16 [32, 1408, 2048], P('fsdp', 'tok'), may hold values from -0.125 to 0.125
- w_down: bfloat16 [32, 1408, 2048], P('fsdp', 'tok'), may hold values from -0.15625 to 0.15625
- grad_out: bfloat16 [2048, 2048], P('fsdp', 'tok'), may hold values from -6 to 6
Outputs:
- layer_out: bfloat16 [2048, 2048], P('fsdp', 'tok')
- d_tokens: bfloat16 [2048, 2048], P('fsdp', 'tok')
- d_gate_probs: float32 [2048, 4], P('fsdp')
- d_w_gate: float32 [32, 1408, 2048], P('fsdp', 'tok')
- d_w_up: float32 [32, 1408, 2048], P('fsdp', 'tok')
- d_w_down: float32 [32, 1408, 2048], P('fsdp', 'tok')
The draws below stay inside these ranges and needn't reach their ends.
Inputs may be any that keep to these rules, and one draw needn't show every extreme that they name: `expert_ids`: each token names 4 different experts. Among the tokens of one index of fsdp (aligned blocks of 128 tokens) no expert is named more than 32 times, a bound that some block reaches.
All inputs are finite; a program needn't handle non-finite values.
Results may differ from the reference program's by a relative error of at most 0.0064.
Values may be sent and summed in bfloat16 or wider, within the bound.
A program may use at most 128 MiB of HBM per device.

```python
import math
import jax
import jax.numpy as jnp
import numpy as np
from jax import lax

D = 2048
H = 1408
TOPK = 4
EXPERTS = 32
TOK_DEV = 128
CAP = 32
TOKENS = 2048
N_FSDP = 16


def steps_of(own_key, shape, pieces, low, largest):
    def one(dim, shards_of):
        steps = jax.random.uniform(jax.random.fold_in(jax.random.fold_in(own_key, 6), dim), (shards_of,), jnp.float32, low / len(pieces), largest / len(pieces))
        return jnp.repeat(jnp.exp(steps), shape[dim] // shards_of).reshape((-1,) + (1,) * (len(shape) - dim - 1))

    loudness = one(*pieces[0])
    for cut in pieces[1:]:
        loudness = loudness * one(*cut)
    return loudness


def shared_out(own_key, own, number, rows, number_of, top, bound, lean):
    order = jax.random.permutation(own_key, number_of)
    crowded, ordinary = shares(number_of, rows * top, bound, lean, True), shares(number_of, rows * top, bound, lean, False)
    places = jnp.arange(number_of)

    def named(tallies, turn):
        used = int((tallies > 0).sum())
        fixed = max(1, used // 4)
        moved = fixed + (places - fixed + turn * (used - fixed)) % max(1, number_of - fixed)
        return jnp.zeros((number_of,), jnp.int32).at[order[jnp.where(places < fixed, places, moved)]].set(jnp.asarray(tallies, jnp.int32))

    tallies = jnp.where(number % 4 == 0, named(crowded, number // 4), named(ordinary, number - number // 4 - 1))
    mixed = jax.random.permutation(jax.random.fold_in(own, 3), number_of)
    source_of, sink = mixed[0:number_of // 2 * 2:2], mixed[1:number_of // 2 * 2:2]
    slack = jnp.minimum(tallies[source_of] - 1, bound - tallies[sink]) // 2
    slack = jnp.where((source_of == order[0]) | (sink == order[0]) | (tallies[sink] == 0), 0, jnp.maximum(slack, 0))
    moved = jax.random.randint(jax.random.fold_in(own, 4), (number_of // 2,), 0, 1 << 20) % (slack + 1)
    tallies = tallies.at[source_of].add(-moved).at[sink].add(moved)
    members = jnp.searchsorted(jnp.cumsum(tallies), jnp.arange(rows * top), side="right").astype(jnp.int32)
    grid = members.reshape(top, rows).T
    grid = grid[jax.random.permutation(jax.random.fold_in(own, 1), rows)]
    turn = jax.random.randint(jax.random.fold_in(own, 2), (rows, 1), 0, top)
    return jnp.take_along_axis(grid, (jnp.arange(top)[None, :] + turn) % top, axis=1)


def shares(amount, total, reach, slope, full):
    loads = [(1 << 20) // math.isqrt(rank ** slope) + 1 for rank in range(1, amount + 1)]
    largest = reach if full else min(reach, max(-(-total // amount), total * loads[0] // sum(loads)))
    least = 1 if total - largest >= amount - 1 else 0
    given, rest = [largest] + [least] * (amount - 1), total - largest - least * (amount - 1)
    while rest > 0:
        movable = [i for i in range(1, amount) if given[i] < largest] or [i for i in range(1, amount) if given[i] < reach]
        pool, remaining = sum([loads[i] for i in movable]), rest
        for i in movable:
            addition = min(reach - given[i], max(1, remaining * loads[i] // pool), rest)
            given[i] = given[i] + addition
            rest = rest - addition
    return np.array(given)


def noise(stream_key, extent, spread, most, split=(), kind=jnp.bfloat16):
    values = spread * jax.random.normal(stream_key, extent, jnp.float32)
    if split:
        values = values * steps_of(stream_key, extent, split, -0.22, 0.18)
    return jnp.clip(values, -most, most).astype(kind)


def setup_inputs(seed: int = 0) -> dict:
    seeds = jax.random.split(jax.random.key(seed), 8)
    tokens = noise(seeds[0], (TOKENS, D), 1.0, 6.0, ((0, 16), (1, 2)))
    expert_ids_keys = jax.random.split(jax.random.fold_in(seeds[1], 1), TOKENS // TOK_DEV)
    expert_ids_turns = jax.random.permutation(jax.random.fold_in(seeds[1], 3), TOKENS // TOK_DEV)
    expert_ids = jax.vmap(lambda own, number: shared_out(jax.random.fold_in(seeds[1], 2), own, number, TOK_DEV, EXPERTS, TOPK, CAP, 2))(expert_ids_keys, expert_ids_turns).reshape((TOKENS, TOPK))
    gate_probs = jnp.clip(jnp.exp(math.log(1.0) - 2.9957323 * jax.random.uniform(seeds[2], (TOKENS, TOPK), jnp.float32) ** steps_of(seeds[2], (TOKENS, TOPK), ((0, 16),), -0.2, 0.2)), 0.05, 1.0)
    w_gate = noise(seeds[3], (EXPERTS, H, D), D ** -0.5, 0.125, ((0, 16), (1, 2)))
    w_up = noise(seeds[4], (EXPERTS, H, D), D ** -0.5, 0.125, ((0, 16), (1, 2)))
    w_down = noise(seeds[5], (EXPERTS, H, D), H ** -0.5, 0.15625, ((0, 16), (1, 2)))
    grad_out = noise(seeds[6], (TOKENS, D), 1.0, 6.0, ((0, 16), (1, 2)))
    return {"tokens": tokens, "expert_ids": expert_ids, "gate_probs": gate_probs, "w_gate": w_gate, "w_up": w_up, "w_down": w_down, "grad_out": grad_out}


def route_slots(expert_ids):
    blocks = expert_ids.reshape(N_FSDP, TOK_DEV * TOPK)
    onehot = (blocks[:, :, None] == jnp.arange(EXPERTS, dtype=jnp.int32)[None, None, :]).astype(jnp.int32)
    position = jnp.sum(jnp.cumsum(onehot, axis=1) * onehot, axis=2) - 1
    block_index = jnp.arange(N_FSDP, dtype=jnp.int32)[:, None]
    slot = blocks * (N_FSDP * CAP) + block_index * CAP + position
    return slot.reshape(-1).astype(jnp.int32)


def expert_pass(operands):
    inputs, weight_gate, weight_up, weight_down, d_out = operands
    gate = jnp.dot(inputs, weight_gate.T, preferred_element_type=jnp.float32)
    upper = jnp.dot(inputs, weight_up.T, preferred_element_type=jnp.float32)
    sigma = jax.nn.sigmoid(gate)
    active = gate * sigma
    hidden = (active * upper).astype(jnp.bfloat16)
    expert_out = jnp.dot(hidden, weight_down, preferred_element_type=jnp.float32).astype(jnp.bfloat16)
    d_hidden = jnp.dot(d_out, weight_down.T, preferred_element_type=jnp.float32)
    d_down = jnp.dot(hidden.T, d_out, preferred_element_type=jnp.float32)
    d_gate = (d_hidden * upper * sigma * (1.0 + gate * (1.0 - sigma))).astype(jnp.bfloat16)
    d_upper = (d_hidden * active).astype(jnp.bfloat16)
    d_wgate = jnp.dot(d_gate.T, inputs, preferred_element_type=jnp.float32)
    d_wup = jnp.dot(d_upper.T, inputs, preferred_element_type=jnp.float32)
    back = jnp.dot(d_gate, weight_gate, preferred_element_type=jnp.float32)
    back = back + jnp.dot(d_upper, weight_up, preferred_element_type=jnp.float32)
    d_inputs = back.astype(jnp.bfloat16)
    return expert_out, d_inputs, d_wgate, d_wup, d_down


def reference(tokens, expert_ids, gate_probs, w_gate, w_up, w_down, grad_out):
    slot = route_slots(expert_ids)
    owner = jnp.arange(TOKENS * TOPK, dtype=jnp.int32) // TOPK
    total = EXPERTS * N_FSDP * CAP
    expert_in = jnp.zeros((total, D), jnp.bfloat16).at[slot].set(tokens[owner]).reshape(EXPERTS, N_FSDP * CAP, D)
    probs = gate_probs[:, :, None]
    scaled = (probs * grad_out[:, None, :].astype(jnp.float32)).astype(jnp.bfloat16).reshape(TOKENS * TOPK, D)
    d_expert_out = jnp.zeros((total, D), jnp.bfloat16).at[slot].set(scaled).reshape(EXPERTS, N_FSDP * CAP, D)
    expert_out, d_expert_in, d_w_gate, d_w_up, d_w_down = lax.map(expert_pass, (expert_in, w_gate, w_up, w_down, d_expert_out))
    route_out = expert_out.reshape(total, D)[slot].reshape(TOKENS, TOPK, D).astype(jnp.float32)
    layer_out = jnp.sum(probs * route_out, axis=1).astype(jnp.bfloat16)
    d_gate_probs = jnp.sum(grad_out[:, None, :].astype(jnp.float32) * route_out, axis=2)
    route_grad = d_expert_in.reshape(total, D)[slot].reshape(TOKENS, TOPK, D).astype(jnp.float32)
    d_tokens = jnp.sum(route_grad, axis=1).astype(jnp.bfloat16)
    return (layer_out, d_tokens, d_gate_probs, d_w_gate, d_w_up, d_w_down)
```

```python
import functools

import jax
import jax.numpy as jnp
from jax import lax
from jax.experimental import pallas as pl
from jax.experimental.pallas import tpu as pltpu
from jax.sharding import PartitionSpec as P

CAP = 32
MESH = pl.DeviceIdType.MESH


def flip(bit, change):
    return 1 - bit if change else bit


class Place:
    def __init__(self):
        f = lax.axis_index("fsdp")
        self.t = lax.axis_index("tok")
        self.core = f % 2
        self.x = (f // 2) % 2
        self.z0 = (f // 4) % 2
        self.z1 = f // 8

    def block(self, dz=0, dx=0, dc=0):
        z = flip(self.z1, dz // 2) * 2 + flip(self.z0, dz % 2)
        return z * 4 + flip(self.x, dx) * 2 + flip(self.core, dc)

    def device(self, dz=0, dx=0, dy=0, dc=0):
        return (self.block(dz, dx, dc), flip(self.t, dy))

    def columns(self, dy, width):
        return pl.ds(pl.multiple_of(flip(self.t, dy) * width, width), width)

    def partners(self):
        return [self.device(dz=d) for d in (1, 2, 3)] + [
            self.device(dx=1),
            self.device(dy=1),
            self.device(dc=1),
        ]


def greet(place):
    barrier = pltpu.get_barrier_semaphore()
    partners = place.partners()
    for partner in partners:
        pl.semaphore_signal(barrier, inc=1, device_id=partner, device_id_type=MESH)
    pl.semaphore_wait(barrier, len(partners))


def gather_kernel(in0, in1, out0, out1, send_sem, recv_sem, core_sem, own_sem):
    place = Place()
    ins, outs = (in0, in1), (out0, out1)
    rows, width = in0.shape
    half = rows // 2
    sent = []

    def where(a, h, dz, dx, dy, dc=0):
        return outs[a].at[
            place.block(dz, dx, dc), pl.ds(h * half, half), place.columns(dy, width)
        ]

    def send(a, h, dz, dx, dy, to, sem):
        own = dz == dx == dy == 0
        source = ins[a].at[pl.ds(h * half, half)] if own else where(a, h, dz, dx, dy)
        copy = pltpu.make_async_remote_copy(
            src_ref=source,
            dst_ref=where(a, h, dz, dx, dy),
            send_sem=send_sem.at[len(sent)],
            recv_sem=sem,
            device_id=to,
            device_id_type=MESH,
        )
        copy.start()
        sent.append(copy)

    def index(a, h, dz, dx, dy):
        return (((a * 2 + h) * 4 + dz) * 2 + dx) * 2 + dy

    def wait(a, h, dz, dx, dy, dc=0):
        place_here = where(a, h, dz, dx, dy, dc)
        sem = (core_sem if dc else recv_sem).at[index(a, h, dz, dx, dy)]
        pltpu.make_async_copy(place_here, place_here, sem).wait()

    def to_core(a, h, dz, dx, dy):
        send(a, h, dz, dx, dy, place.device(dc=1), core_sem.at[index(a, h, dz, dx, dy)])

    def to_x(a, h, dz, dy):
        send(a, h, dz, 0, dy, place.device(dx=1), recv_sem.at[index(a, h, dz, 1, dy)])

    def to_y(a, h, dz, dx):
        send(a, h, dz, dx, 0, place.device(dy=1), recv_sem.at[index(a, h, dz, dx, 1)])

    own_copies = [
        pltpu.make_async_copy(
            ins[a], outs[a].at[place.block(), :, place.columns(0, width)], own_sem.at[a]
        )
        for a in range(2)
    ]
    for copy in own_copies:
        copy.start()
    greet(place)
    events = []
    for a in range(2):
        for h in range(2):
            for dz in range(1, 4):
                events.append((a * 3, "z", a, h, dz))
            for dz in range(4):
                events.append((a * 30 + dz * 5 + 1, "column", a, h, dz))
                events.append((a * 30 + dz * 5 + 12, "plane", a, h, dz))
                events.append((a * 30 + dz * 5 + 22, "last", a, h, dz))
    for _, kind, a, h, dz in sorted(events):
        if kind == "z":
            send(a, h, 0, 0, 0, place.device(dz=dz), recv_sem.at[index(a, h, dz, 0, 0)])
        elif kind == "column":
            if dz:
                wait(a, h, dz, 0, 0)
            if h == 0:
                to_x(a, h, dz, 0)
                to_y(a, h, dz, 0)
            else:
                to_y(a, h, dz, 0)
                to_x(a, h, dz, 0)
            to_core(a, h, dz, 0, 0)
        elif kind == "plane":
            if h == 0:
                wait(a, h, dz, 1, 0)
                to_y(a, h, dz, 1)
                to_core(a, h, dz, 1, 0)
            else:
                wait(a, h, dz, 0, 1)
                to_x(a, h, dz, 1)
                to_core(a, h, dz, 0, 1)
        else:
            dx, dy = (0, 1) if h == 0 else (1, 0)
            wait(a, h, dz, dx, dy)
            to_core(a, h, dz, dx, dy)
            wait(a, h, dz, 1, 1)
            to_core(a, h, dz, 1, 1)
    for a in range(2):
        for h in range(2):
            for dz in range(4):
                for dx in range(2):
                    for dy in range(2):
                        wait(a, h, dz, dx, dy, 1)
    for copy in sent:
        copy.wait_send()
    for copy in own_copies:
        copy.wait()


def gather_pair(first, second):
    rows, width = first.shape
    full = jax.ShapeDtypeStruct((16, rows, 2 * width), first.dtype)
    return pl.pallas_call(
        gather_kernel,
        out_shape=(full, full),
        in_specs=[pl.BlockSpec(memory_space=pl.ANY)] * 2,
        out_specs=[pl.BlockSpec(memory_space=pl.ANY)] * 2,
        scratch_shapes=[
            pltpu.SemaphoreType.DMA((124,)),
            pltpu.SemaphoreType.DMA((64,)),
            pltpu.SemaphoreType.DMA((64,)),
            pltpu.SemaphoreType.DMA((2,)),
        ],
        compiler_params=pltpu.CompilerParams(collective_id=0, has_side_effects=True),
    )(first, second)


def scatter_kernel(
    in0, in1, out0, out1, core_buf, wide_buf, near_buf, z_buf, send_sem, core_sem, wide_sem, near_sem, z_sem
):
    place = Place()
    ins, outs = (in0, in1), (out0, out1)
    half, width = core_buf.shape[-2:]
    sent = []

    def send(source, target, sem, to):
        copy = pltpu.make_async_remote_copy(
            src_ref=source,
            dst_ref=target,
            send_sem=send_sem.at[len(sent)],
            recv_sem=sem,
            device_id=to,
            device_id_type=MESH,
        )
        copy.start()
        sent.append(copy)

    def arrive(buffer, sem):
        pltpu.make_async_copy(buffer, buffer, sem).wait()

    def add(target, source):
        def step(i, carry):
            at = pl.ds(pl.multiple_of(i * 16, 16), 16)
            target[at, :] = target[at, :] + source[at, :]
            return carry

        lax.fori_loop(0, half // 16, step, 0)

    def part(a, h, dz, dx, dy, dc):
        return ins[a].at[
            place.block(dz, dx, dc), pl.ds(h * half, half), place.columns(dy, width)
        ]

    def slot(a, h, dz, dx, dy):
        return (((a * 2 + h) * 4 + dz) * 2 + dx) * 2 + dy

    greet(place)
    order = [3, 2, 1, 0]
    events = []
    for a in range(2):
        for n, dz in enumerate(order):
            for h in range(2):
                events.append((a * 30 + n * 2 - 40, "core", a, h, dz))
                events.append((a * 30 + n * 6 + 4, "wide", a, h, dz))
                events.append((a * 30 + n * 6 + 14, "near", a, h, dz))
                events.append((a * 30 + n * 6 + 22, "z", a, h, dz))
    for _, kind, a, h, dz in sorted(events):
        pair = (a * 2 + h) * 4 + dz
        across = place.device(dy=1) if h == 0 else place.device(dx=1)
        along = place.device(dx=1) if h == 0 else place.device(dy=1)
        if kind == "core":
            for far in (1, 0):
                for other in (1, 0):
                    dx, dy = (other, far) if h == 0 else (far, other)
                    k = slot(a, h, dz, dx, dy)
                    send(part(a, h, dz, dx, dy, 1), core_buf.at[k], core_sem.at[k], place.device(dc=1))
        elif kind == "wide":
            for far in (1, 0):
                for other in (1, 0):
                    dx, dy = (other, far) if h == 0 else (far, other)
                    k = slot(a, h, dz, dx, dy)
                    arrive(core_buf.at[k], core_sem.at[k])
                    add(core_buf.at[k], part(a, h, dz, dx, dy, 0))
                    if far:
                        w = pair * 2 + other
                        send(core_buf.at[k], wide_buf.at[w], wide_sem.at[w], across)
        elif kind == "near":
            for other in (1, 0):
                dx, dy = (other, 0) if h == 0 else (0, other)
                w = pair * 2 + other
                arrive(wide_buf.at[w], wide_sem.at[w])
                add(wide_buf.at[w], core_buf.at[slot(a, h, dz, dx, dy)])
                if other:
                    send(wide_buf.at[w], near_buf.at[pair], near_sem.at[pair], along)
        else:
            arrive(near_buf.at[pair], near_sem.at[pair])
            add(near_buf.at[pair], wide_buf.at[pair * 2])
            if dz:
                send(near_buf.at[pair], z_buf.at[pair], z_sem.at[pair], place.device(dz=dz))
    for a in range(2):
        for h in range(2):
            pair = (a * 2 + h) * 4
            for dz in (3, 2, 1):
                arrive(z_buf.at[pair + dz], z_sem.at[pair + dz])

            def step(i, carry, a=a, h=h, pair=pair):
                at = pl.ds(pl.multiple_of(i * 16, 16), 16)
                total = near_buf[pair, at, :].astype(jnp.float32)
                for dz in (1, 2, 3):
                    total = total + z_buf[pair + dz, at, :].astype(jnp.float32)
                to = pl.ds(pl.multiple_of(h * half + i * 16, 16), 16)
                outs[a][to, :] = total.astype(outs[a].dtype)
                return carry

            lax.fori_loop(0, half // 16, step, 0)
    for copy in sent:
        copy.wait_send()


def scatter_pair(first, second):
    blocks, rows, full = first.shape
    half, width = rows // 2, full // 2
    out = jax.ShapeDtypeStruct((rows, width), first.dtype)
    return pl.pallas_call(
        scatter_kernel,
        out_shape=(out, out),
        in_specs=[pl.BlockSpec(memory_space=pltpu.VMEM)] * 2,
        out_specs=[pl.BlockSpec(memory_space=pltpu.VMEM)] * 2,
        scratch_shapes=[
            pltpu.VMEM((64, half, width), first.dtype),
            pltpu.VMEM((32, half, width), first.dtype),
            pltpu.VMEM((16, half, width), first.dtype),
            pltpu.VMEM((16, half, width), first.dtype),
            pltpu.SemaphoreType.DMA((124,)),
            pltpu.SemaphoreType.DMA((64,)),
            pltpu.SemaphoreType.DMA((32,)),
            pltpu.SemaphoreType.DMA((16,)),
            pltpu.SemaphoreType.DMA((16,)),
        ],
        compiler_params=pltpu.CompilerParams(
            collective_id=1, has_side_effects=True, vmem_limit_bytes=48 * 2**20
        ),
    )(first, second)


def gather_any(value):
    wide = lax.all_gather(value, "tok", axis=1, tiled=True)
    return lax.all_gather(wide, "fsdp", axis=0, tiled=False)


def scatter_any(value):
    blocks, rows, full = value.shape
    mine = lax.psum_scatter(
        value.reshape(blocks * rows, full), "fsdp", scatter_dimension=0, tiled=True
    )
    return lax.psum_scatter(mine, "tok", scatter_dimension=1, tiled=True)


def on_device(by_kernel, tokens, expert_ids, gate_probs, w_gate, w_up, w_down, grad_out):
    tok_rows, topk = expert_ids.shape
    local = w_gate.shape[0]
    f32 = jnp.float32
    me = lax.axis_index("fsdp")

    routes = jnp.concatenate([expert_ids.astype(f32).T, gate_probs.T], axis=0)
    routes = lax.all_gather(routes, "fsdp", axis=0, tiled=False)
    if by_kernel:
        all_tokens, all_grads = gather_pair(tokens, grad_out)
    else:
        all_tokens, all_grads = gather_any(tokens), gather_any(grad_out)
    blocks = all_tokens.shape[0]

    names = routes[:, :topk]
    mine = (me * local + jnp.arange(local, dtype=jnp.int32)).astype(f32)
    chosen = names[None] == mine[:, None, None, None]
    hit = jnp.any(chosen, axis=2)
    prob = jnp.sum(jnp.where(chosen, routes[None, :, topk:], 0.0), axis=2)
    before = jnp.triu(jnp.ones((tok_rows, tok_rows), jnp.bfloat16), 1)
    place = jnp.einsum("ebs,st->ebt", hit.astype(jnp.bfloat16), before, preferred_element_type=f32)
    place = jnp.where(hit, place, -1.0)
    filled = place[:, :, None, :] == jnp.arange(CAP, dtype=jnp.int32).astype(f32)[None, None, :, None]
    select = filled.astype(jnp.bfloat16)
    row_prob = jnp.sum(jnp.where(filled, prob[:, :, None, :], 0.0), axis=3)
    row_prob = row_prob.reshape(local, blocks * CAP, 1)

    def pick(values):
        rows = jnp.einsum("ebrt,btd->ebrd", select, values, preferred_element_type=f32)
        return rows.astype(jnp.bfloat16).reshape(local, blocks * CAP, values.shape[-1])

    def place_back(rows):
        rows = rows.astype(jnp.bfloat16).reshape(local, blocks, CAP, rows.shape[-1])
        values = jnp.einsum("ebrt,ebrd->btd", select, rows, preferred_element_type=f32)
        return values.astype(jnp.bfloat16)

    inputs = pick(all_tokens)
    cotangent = pick(all_grads)
    gate = jnp.einsum("erd,ehd->erh", inputs, w_gate, preferred_element_type=f32)
    upper = jnp.einsum("erd,ehd->erh", inputs, w_up, preferred_element_type=f32)
    raw = jnp.einsum("erd,ehd->erh", cotangent, w_down, preferred_element_type=f32)
    sigma = jax.nn.sigmoid(gate)
    active = gate * sigma
    hidden = active * upper
    weighted = (row_prob * hidden).astype(jnp.bfloat16)
    d_hidden = row_prob * raw
    d_gate = (d_hidden * upper * sigma * (1.0 + gate * (1.0 - sigma))).astype(jnp.bfloat16)
    d_upper = (d_hidden * active).astype(jnp.bfloat16)
    d_rows = jnp.sum(hidden * raw, axis=2).reshape(local, blocks, CAP)

    out_rows = jnp.einsum("erh,ehd->erd", weighted, w_down, preferred_element_type=f32)
    in_rows = jnp.einsum("erh,ehd->erd", d_gate, w_gate, preferred_element_type=f32)
    in_rows = in_rows + jnp.einsum("erh,ehd->erd", d_upper, w_up, preferred_element_type=f32)
    part_out, part_in = place_back(out_rows), place_back(in_rows)
    if by_kernel:
        layer_out, d_tokens = scatter_pair(part_out, part_in)
    else:
        layer_out, d_tokens = scatter_any(part_out), scatter_any(part_in)

    d_w_down = jnp.einsum("erh,erd->ehd", weighted, cotangent, preferred_element_type=f32)
    d_w_gate = jnp.einsum("erh,erd->ehd", d_gate, inputs, preferred_element_type=f32)
    d_w_up = jnp.einsum("erh,erd->ehd", d_upper, inputs, preferred_element_type=f32)

    d_prob = jnp.sum(jnp.where(filled, d_rows[:, :, :, None], 0.0), axis=2)
    d_prob = jnp.sum(jnp.where(chosen, d_prob[:, :, None, :], 0.0), axis=0)
    d_prob = lax.psum(d_prob.reshape(blocks, topk * tok_rows), ("fsdp", "tok"))
    d_prob = lax.dynamic_index_in_dim(d_prob, me, 0, keepdims=False)
    d_gate_probs = d_prob.reshape(topk, tok_rows).T
    return (layer_out, d_tokens, d_gate_probs, d_w_gate, d_w_up, d_w_down)


def solution(mesh):
    by_kernel = mesh.shape["fsdp"] == 16 and mesh.shape["tok"] == 2
    return jax.shard_map(
        functools.partial(on_device, by_kernel),
        mesh=mesh,
        in_specs=(
            P("fsdp", "tok"),
            P("fsdp", None),
            P("fsdp", None),
            P("fsdp", "tok", None),
            P("fsdp", "tok", None),
            P("fsdp", "tok", None),
            P("fsdp", "tok"),
        ),
        out_specs=(
            P("fsdp", "tok"),
            P("fsdp", "tok"),
            P("fsdp", None),
            P("fsdp", "tok", None),
            P("fsdp", "tok", None),
            P("fsdp", "tok", None),
        ),
        check_vma=False,
    )
```

```python
import functools

import jax
import jax.numpy as jnp
from jax import lax
from jax.experimental import pallas as pl
from jax.experimental.pallas import tpu as pltpu
from jax.sharding import PartitionSpec as P

CAP = 32
MESH = pl.DeviceIdType.MESH


def flip(bit, change):
    return 1 - bit if change else bit


class Place:
    def __init__(self):
        f = lax.axis_index("fsdp")
        self.t = lax.axis_index("tok")
        self.core = f % 2
        self.x = (f // 2) % 2
        self.z0 = (f // 4) % 2
        self.z1 = f // 8

    def block(self, dz=0, dx=0, dc=0):
        z = flip(self.z1, dz // 2) * 2 + flip(self.z0, dz % 2)
        return z * 4 + flip(self.x, dx) * 2 + flip(self.core, dc)

    def device(self, dz=0, dx=0, dy=0, dc=0):
        return (self.block(dz, dx, dc), flip(self.t, dy))

    def columns(self, dy, width):
        return pl.ds(pl.multiple_of(flip(self.t, dy) * width, width), width)

    def partners(self):
        return [self.device(dz=d) for d in (1, 2, 3)] + [
            self.device(dx=1),
            self.device(dy=1),
            self.device(dc=1),
        ]


def greet(place):
    barrier = pltpu.get_barrier_semaphore()
    partners = place.partners()
    for partner in partners:
        pl.semaphore_signal(barrier, inc=1, device_id=partner, device_id_type=MESH)
    pl.semaphore_wait(barrier, len(partners))


def gather_kernel(in0, in1, out0, out1, send_sem, recv_sem, core_sem, own_sem):
    place = Place()
    ins, outs = (in0, in1), (out0, out1)
    rows, width = in0.shape
    half = rows // 2
    sent = []

    def where(a, h, dz, dx, dy, dc=0):
        return outs[a].at[
            place.block(dz, dx, dc), pl.ds(h * half, half), place.columns(dy, width)
        ]

    def send(a, h, dz, dx, dy, to, sem):
        own = dz == dx == dy == 0
        source = ins[a].at[pl.ds(h * half, half)] if own else where(a, h, dz, dx, dy)
        copy = pltpu.make_async_remote_copy(
            src_ref=source,
            dst_ref=where(a, h, dz, dx, dy),
            send_sem=send_sem.at[len(sent)],
            recv_sem=sem,
            device_id=to,
            device_id_type=MESH,
        )
        copy.start()
        sent.append(copy)

    def index(a, h, dz, dx, dy):
        return (((a * 2 + h) * 4 + dz) * 2 + dx) * 2 + dy

    def wait(a, h, dz, dx, dy, dc=0):
        place_here = where(a, h, dz, dx, dy, dc)
        sem = (core_sem if dc else recv_sem).at[index(a, h, dz, dx, dy)]
        pltpu.make_async_copy(place_here, place_here, sem).wait()

    def to_core(a, h, dz, dx, dy):
        send(a, h, dz, dx, dy, place.device(dc=1), core_sem.at[index(a, h, dz, dx, dy)])

    def to_x(a, h, dz, dy):
        send(a, h, dz, 0, dy, place.device(dx=1), recv_sem.at[index(a, h, dz, 1, dy)])

    def to_y(a, h, dz, dx):
        send(a, h, dz, dx, 0, place.device(dy=1), recv_sem.at[index(a, h, dz, dx, 1)])

    own_copies = [
        pltpu.make_async_copy(
            ins[a], outs[a].at[place.block(), :, place.columns(0, width)], own_sem.at[a]
        )
        for a in range(2)
    ]
    for copy in own_copies:
        copy.start()
    greet(place)
    events = []
    for a in range(2):
        for h in range(2):
            for dz in range(1, 4):
                events.append((a * 3, "z", a, h, dz))
            for dz in range(4):
                events.append((a * 30 + dz * 5 + 1, "column", a, h, dz))
                events.append((a * 30 + dz * 5 + 12, "plane", a, h, dz))
                events.append((a * 30 + dz * 5 + 22, "last", a, h, dz))
    for _, kind, a, h, dz in sorted(events):
        if kind == "z":
            send(a, h, 0, 0, 0, place.device(dz=dz), recv_sem.at[index(a, h, dz, 0, 0)])
        elif kind == "column":
            if dz:
                wait(a, h, dz, 0, 0)
            if h == 0:
                to_x(a, h, dz, 0)
                to_y(a, h, dz, 0)
            else:
                to_y(a, h, dz, 0)
                to_x(a, h, dz, 0)
            to_core(a, h, dz, 0, 0)
        elif kind == "plane":
            if h == 0:
                wait(a, h, dz, 1, 0)
                to_y(a, h, dz, 1)
                to_core(a, h, dz, 1, 0)
            else:
                wait(a, h, dz, 0, 1)
                to_x(a, h, dz, 1)
                to_core(a, h, dz, 0, 1)
        else:
            dx, dy = (0, 1) if h == 0 else (1, 0)
            wait(a, h, dz, dx, dy)
            to_core(a, h, dz, dx, dy)
            wait(a, h, dz, 1, 1)
            to_core(a, h, dz, 1, 1)
    for a in range(2):
        for h in range(2):
            for dz in range(4):
                for dx in range(2):
                    for dy in range(2):
                        wait(a, h, dz, dx, dy, 1)
    for copy in sent:
        copy.wait_send()
    for copy in own_copies:
        copy.wait()


def gather_pair(first, second):
    rows, width = first.shape
    full = jax.ShapeDtypeStruct((16, rows, 2 * width), first.dtype)
    return pl.pallas_call(
        gather_kernel,
        out_shape=(full, full),
        in_specs=[pl.BlockSpec(memory_space=pl.ANY)] * 2,
        out_specs=[pl.BlockSpec(memory_space=pl.ANY)] * 2,
        scratch_shapes=[
            pltpu.SemaphoreType.DMA((124,)),
            pltpu.SemaphoreType.DMA((64,)),
            pltpu.SemaphoreType.DMA((64,)),
            pltpu.SemaphoreType.DMA((2,)),
        ],
        compiler_params=pltpu.CompilerParams(collective_id=0, has_side_effects=True),
    )(first, second)


def scatter_kernel(
    in0, in1, out0, out1, core_buf, wide_buf, near_buf, z_buf, send_sem, core_sem, wide_sem, near_sem, z_sem
):
    place = Place()
    ins, outs = (in0, in1), (out0, out1)
    half, width = core_buf.shape[-2:]
    sent = []

    def send(source, target, sem, to):
        copy = pltpu.make_async_remote_copy(
            src_ref=source,
            dst_ref=target,
            send_sem=send_sem.at[len(sent)],
            recv_sem=sem,
            device_id=to,
            device_id_type=MESH,
        )
        copy.start()
        sent.append(copy)

    def arrive(buffer, sem):
        pltpu.make_async_copy(buffer, buffer, sem).wait()

    def add(target, source):
        def step(i, carry):
            at = pl.ds(pl.multiple_of(i * 16, 16), 16)
            target[at, :] = target[at, :] + source[at, :]
            return carry

        lax.fori_loop(0, half // 16, step, 0)

    def part(a, h, dz, dx, dy, dc):
        return ins[a].at[
            place.block(dz, dx, dc), pl.ds(h * half, half), place.columns(dy, width)
        ]

    def slot(a, h, dz, dx, dy):
        return (((a * 2 + h) * 4 + dz) * 2 + dx) * 2 + dy

    greet(place)
    order = [3, 2, 1, 0]
    events = []
    for a in range(2):
        for n, dz in enumerate(order):
            for h in range(2):
                events.append((a * 30 + n * 2 - 40, "core", a, h, dz))
                events.append((a * 30 + n * 6 + 4, "wide", a, h, dz))
                events.append((a * 30 + n * 6 + 14, "near", a, h, dz))
                events.append((a * 30 + n * 6 + 22, "z", a, h, dz))
    for _, kind, a, h, dz in sorted(events):
        pair = (a * 2 + h) * 4 + dz
        across = place.device(dy=1) if h == 0 else place.device(dx=1)
        along = place.device(dx=1) if h == 0 else place.device(dy=1)
        if kind == "core":
            for far in (1, 0):
                for other in (1, 0):
                    dx, dy = (other, far) if h == 0 else (far, other)
                    k = slot(a, h, dz, dx, dy)
                    send(part(a, h, dz, dx, dy, 1), core_buf.at[k], core_sem.at[k], place.device(dc=1))
        elif kind == "wide":
            for far in (1, 0):
                for other in (1, 0):
                    dx, dy = (other, far) if h == 0 else (far, other)
                    k = slot(a, h, dz, dx, dy)
                    arrive(core_buf.at[k], core_sem.at[k])
                    add(core_buf.at[k], part(a, h, dz, dx, dy, 0))
                    if far:
                        w = pair * 2 + other
                        send(core_buf.at[k], wide_buf.at[w], wide_sem.at[w], across)
        elif kind == "near":
            for other in (1, 0):
                dx, dy = (other, 0) if h == 0 else (0, other)
                w = pair * 2 + other
                arrive(wide_buf.at[w], wide_sem.at[w])
                add(wide_buf.at[w], core_buf.at[slot(a, h, dz, dx, dy)])
                if other:
                    send(wide_buf.at[w], near_buf.at[pair], near_sem.at[pair], along)
        else:
            arrive(near_buf.at[pair], near_sem.at[pair])
            add(near_buf.at[pair], wide_buf.at[pair * 2])
            if dz:
                send(near_buf.at[pair], z_buf.at[pair], z_sem.at[pair], place.device(dz=dz))
    for a in range(2):
        for h in range(2):
            pair = (a * 2 + h) * 4
            for dz in (3, 2, 1):
                arrive(z_buf.at[pair + dz], z_sem.at[pair + dz])

            def step(i, carry, a=a, h=h, pair=pair):
                at = pl.ds(pl.multiple_of(i * 16, 16), 16)
                total = near_buf[pair, at, :].astype(jnp.float32)
                for dz in (1, 2, 3):
                    total = total + z_buf[pair + dz, at, :].astype(jnp.float32)
                to = pl.ds(pl.multiple_of(h * half + i * 16, 16), 16)
                outs[a][to, :] = total.astype(outs[a].dtype)
                return carry

            lax.fori_loop(0, half // 16, step, 0)
    for copy in sent:
        copy.wait_send()


def scatter_pair(first, second):
    blocks, rows, full = first.shape
    half, width = rows // 2, full // 2
    out = jax.ShapeDtypeStruct((rows, width), first.dtype)
    return pl.pallas_call(
        scatter_kernel,
        out_shape=(out, out),
        in_specs=[pl.BlockSpec(memory_space=pltpu.VMEM)] * 2,
        out_specs=[pl.BlockSpec(memory_space=pltpu.VMEM)] * 2,
        scratch_shapes=[
            pltpu.VMEM((64, half, width), first.dtype),
            pltpu.VMEM((32, half, width), first.dtype),
            pltpu.VMEM((16, half, width), first.dtype),
            pltpu.VMEM((16, half, width), first.dtype),
            pltpu.SemaphoreType.DMA((124,)),
            pltpu.SemaphoreType.DMA((64,)),
            pltpu.SemaphoreType.DMA((32,)),
            pltpu.SemaphoreType.DMA((16,)),
            pltpu.SemaphoreType.DMA((16,)),
        ],
        compiler_params=pltpu.CompilerParams(
            collective_id=1, has_side_effects=True, vmem_limit_bytes=48 * 2**20
        ),
    )(first, second)


def gather_any(value):
    wide = lax.all_gather(value, "tok", axis=1, tiled=True)
    return lax.all_gather(wide, "fsdp", axis=0, tiled=False)


def scatter_any(value):
    blocks, rows, full = value.shape
    mine = lax.psum_scatter(
        value.reshape(blocks * rows, full), "fsdp", scatter_dimension=0, tiled=True
    )
    return lax.psum_scatter(mine, "tok", scatter_dimension=1, tiled=True)


def on_device(by_kernel, tokens, expert_ids, gate_probs, w_gate, w_up, w_down, grad_out):
    tok_rows, topk = expert_ids.shape
    local = w_gate.shape[0]
    f32 = jnp.float32
    me = lax.axis_index("fsdp")

    routes = jnp.concatenate([expert_ids.astype(f32).T, gate_probs.T], axis=0)
    routes = lax.all_gather(routes, "fsdp", axis=0, tiled=False)
    if by_kernel:
        all_tokens, all_grads = gather_pair(tokens, grad_out)
    else:
        all_tokens, all_grads = gather_any(tokens), gather_any(grad_out)
    blocks = all_tokens.shape[0]

    names = routes[:, :topk]
    mine = (me * local + jnp.arange(local, dtype=jnp.int32)).astype(f32)
    chosen = names[None] == mine[:, None, None, None]
    hit = jnp.any(chosen, axis=2)
    prob = jnp.sum(jnp.where(chosen, routes[None, :, topk:], 0.0), axis=2)
    before = jnp.triu(jnp.ones((tok_rows, tok_rows), jnp.bfloat16), 1)
    place = jnp.einsum("ebs,st->ebt", hit.astype(jnp.bfloat16), before, preferred_element_type=f32)
    place = jnp.where(hit, place, -1.0)
    filled = place[:, :, None, :] == jnp.arange(CAP, dtype=jnp.int32).astype(f32)[None, None, :, None]
    select = filled.astype(jnp.bfloat16)
    row_prob = jnp.sum(jnp.where(filled, prob[:, :, None, :], 0.0), axis=3)
    row_prob = row_prob.reshape(local, blocks * CAP, 1)

    def pick(values):
        rows = jnp.einsum("ebrt,btd->ebrd", select, values, preferred_element_type=f32)
        return rows.astype(jnp.bfloat16).reshape(local, blocks * CAP, values.shape[-1])

    def place_back(rows):
        rows = rows.astype(jnp.bfloat16).reshape(local, blocks, CAP, rows.shape[-1])
        values = jnp.einsum("ebrt,ebrd->btd", select, rows, preferred_element_type=f32)
        return values.astype(jnp.bfloat16)

    inputs = pick(all_tokens)
    cotangent = pick(all_grads)
    gate = jnp.einsum("erd,ehd->erh", inputs, w_gate, preferred_element_type=f32)
    upper = jnp.einsum("erd,ehd->erh", inputs, w_up, preferred_element_type=f32)
    raw = jnp.einsum("erd,ehd->erh", cotangent, w_down, preferred_element_type=f32)
    sigma = jax.nn.sigmoid(gate)
    active = gate * sigma
    hidden = active * upper
    weighted = (row_prob * hidden).astype(jnp.bfloat16)
    d_hidden = row_prob * raw
    d_gate = (d_hidden * upper * sigma * (1.0 + gate * (1.0 - sigma))).astype(jnp.bfloat16)
    d_upper = (d_hidden * active).astype(jnp.bfloat16)
    d_rows = jnp.sum(hidden * raw, axis=2).reshape(local, blocks, CAP)

    out_rows = jnp.einsum("erh,ehd->erd", weighted, w_down, preferred_element_type=f32)
    in_rows = jnp.einsum("erh,ehd->erd", d_gate, w_gate, preferred_element_type=f32)
    in_rows = in_rows + jnp.einsum("erh,ehd->erd", d_upper, w_up, preferred_element_type=f32)
    part_out, part_in = place_back(out_rows), place_back(in_rows)
    if by_kernel:
        layer_out, d_tokens = scatter_pair(part_out, part_in)
    else:
        layer_out, d_tokens = scatter_any(part_out), scatter_any(part_in)

    d_w_down = jnp.einsum("erh,erd->ehd", weighted, cotangent, preferred_element_type=f32)
    d_w_gate = jnp.einsum("erh,erd->ehd", d_gate, inputs, preferred_element_type=f32)
    d_w_up = jnp.einsum("erh,erd->ehd", d_upper, inputs, preferred_element_type=f32)

    d_prob = jnp.sum(jnp.where(filled, d_rows[:, :, :, None], 0.0), axis=2)
    d_prob = jnp.sum(jnp.where(chosen, d_prob[:, :, None, :], 0.0), axis=0)
    d_prob = d_prob.reshape(blocks, topk * tok_rows)
    d_prob = lax.all_to_all(d_prob, "fsdp", split_axis=0, concat_axis=0, tiled=True)
    d_prob = jnp.sum(d_prob, axis=0)
    size = lax.axis_size("tok")
    mine_only = d_prob
    for turn in range(1, size):
        pairs = [(i, (i + turn) % size) for i in range(size)]
        d_prob = d_prob + lax.ppermute(mine_only, "tok", pairs)
    d_gate_probs = d_prob.reshape(topk, tok_rows).T
    return (layer_out, d_tokens, d_gate_probs, d_w_gate, d_w_up, d_w_down)


def solution(mesh):
    by_kernel = mesh.shape["fsdp"] == 16 and mesh.shape["tok"] == 2
    return jax.shard_map(
        functools.partial(on_device, by_kernel),
        mesh=mesh,
        in_specs=(
            P("fsdp", "tok"),
            P("fsdp", None),
            P("fsdp", None),
            P("fsdp", "tok", None),
            P("fsdp", "tok", None),
            P("fsdp", "tok", None),
            P("fsdp", "tok"),
        ),
        out_specs=(
            P("fsdp", "tok"),
            P("fsdp", "tok"),
            P("fsdp", None),
            P("fsdp", "tok", None),
            P("fsdp", "tok", None),
            P("fsdp", "tok", None),
        ),
        check_vma=False,
    )
```
